256 devices in a mesh: seq: 32 (over z, x), head: 8 (over y, core).
Axes of the slice: x: 4, y: 4, z: 8, core: 2. Of those that a mesh axis runs over, the one named last changes fastest.
Arguments:
- queries: bfloat16 [16384, 6144], P('seq', 'head'), may hold values from -0.5 to 0.5
- keys: bfloat16 [16384, 6144], P('seq', 'head'), may hold values from -0.5 to 0.5
- values: bfloat16 [16384, 6144], P('seq', 'head'), may hold values from -6 to 6
- doc_lengths: int32 [32], replicated, may hold values from 1 to 12288, 16384 in all
- decay_rates: float32 [48], P('head'), may hold values from 1.8310548e-05 to 0.06
- gain: float32 [6144], P('head'), may hold values from 0.5 to 1.5
- out_grad: bfloat16 [16384, 6144], P('seq', 'head'), may hold values from -6 to 6
Outputs:
- grad_queries: bfloat16 [16384, 6144], P('seq', 'head')
- grad_keys: bfloat16 [16384, 6144], P('seq', 'head')
- grad_values: bfloat16 [16384, 6144], P('seq', 'head')
- gain_grad: float32 [6144], P('head')
The draws below stay inside these ranges and needn't reach their ends.
Inputs may be any that keep to these rules, and one draw needn't show every extreme that they name: `doc_lengths`: document lengths in order; they sum to 16384 and the longest is exactly 12288.
All inputs are finite; a program needn't handle non-finite values.
Results may differ from the reference program's by a relative error of at most 0.013.
Values may be sent and summed in bfloat16 or wider, within the bound.
A program may use at most 128 MiB of HBM per device.

```python
import math
import jax
import jax.numpy as jnp
import numpy as np
from jax import lax

HEAD_SIZE = 128
TOK_DEV = 512
HEADS = 48
TOKENS = 16384
DOCS = 32
N_SEQ = 32


def steps_of(key, shape, shards, least, high):
    def one(dim, parts):
        draws = jax.random.uniform(jax.random.fold_in(jax.random.fold_in(key, 6), dim), (parts,), jnp.float32, least / len(shards), high / len(shards))
        return jnp.repeat(jnp.exp(draws), shape[dim] // parts).reshape((-1,) + (1,) * (len(shape) - dim - 1))

    level = one(*shards[0])
    for cut in shards[1:]:
        level = level * one(*cut)
    return level


def profile(count, total, most, lean):
    loads = [(1 << 20) // math.isqrt(grade ** lean) + 1 for grade in range(2, count + 1)]
    spare, holding = total - most - (count - 1), [1] * (count - 1)
    while spare > 0:
        candidates = [i for i in range(count - 1) if holding[i] < most]
        mass, budget = sum([loads[i] for i in candidates]), spare
        for i in candidates:
            addition = min(most - holding[i], max(1, budget * loads[i] // mass), spare)
            holding[i] = holding[i] + addition
            spare = spare - addition
    return np.array([most] + holding)


def uneven(stream_key, count, total, reach, skew):
    if count == 2:
        one = jax.random.randint(stream_key, (), max(1, total - reach), min(reach, total - 1) + 1)
        return jnp.stack([one, total - one])
    tallies = jnp.asarray(profile(count, total, reach, skew), jnp.int32)
    pairs = (count - 1) // 2
    source_of, receiver = tallies[1:1 + 2 * pairs:2], tallies[2:2 + 2 * pairs:2]
    slack = jnp.minimum(source_of - 1, reach - receiver)
    moved = jax.random.randint(jax.random.fold_in(stream_key, 1), (pairs,), 0, 1 << 20) % (slack + 1)
    tallies = tallies.at[1:1 + 2 * pairs:2].set(source_of - moved).at[2:2 + 2 * pairs:2].set(receiver + moved)
    return tallies[jax.random.permutation(jax.random.fold_in(stream_key, 2), count)]


def bell_draw(rng, shape, deviation, limit, cuts=(), kind=jnp.bfloat16):
    level = steps_of(rng, shape, cuts, -0.22, 0.18) if cuts else 1.0
    values = jax.random.normal(rng, shape, jnp.float32) * deviation * level
    return jnp.minimum(jnp.maximum(values, -limit), limit).astype(kind)


def setup_inputs(seed: int = 0) -> dict:
    key_of = jax.random.split(jax.random.key(seed), 8)
    return {
        "queries": bell_draw(key_of[0], (TOKENS, HEADS * HEAD_SIZE), 0.09, 0.5, ((0, 32), (1, 8))),
        "keys": bell_draw(key_of[1], (TOKENS, HEADS * HEAD_SIZE), 0.09, 0.5, ((0, 32), (1, 8))),
        "values": bell_draw(key_of[2], (TOKENS, HEADS * HEAD_SIZE), 1.0, 6.0, ((0, 32), (1, 8))),
        "doc_lengths": uneven(key_of[3], DOCS, TOKENS, 3 * TOKENS // 4, 2).astype(jnp.int32),
        "decay_rates": jnp.clip(jnp.exp(math.log(0.06) - 8.094623 * jax.random.uniform(key_of[4], (HEADS,), jnp.float32) ** steps_of(key_of[4], (HEADS,), ((0, 8),), -0.2, 0.2)), 1.831054760259576e-05, 0.06),
        "gain": jnp.clip(1.0 + 0.1 * jax.random.normal(key_of[5], (HEADS * HEAD_SIZE,), jnp.float32), 0.5, 1.5),
        "out_grad": bell_draw(key_of[6], (TOKENS, HEADS * HEAD_SIZE), 1.0, 6.0, ((0, 32), (1, 8))),
    }


EPS = 1e-06

def doc_index(ends, positions):
    return lax.optimization_barrier(jnp.sum((ends[None, :] <= positions[:, None]).astype(jnp.int32), axis=1))

def head_tables(rate, seg_tok, prev_seg, last_seg, count, nblocks):
    upos = jnp.arange(count).astype(jnp.float32)
    first = (seg_tok == prev_seg[:, None]).astype(jnp.float32)
    final = (seg_tok == last_seg[:, None]).astype(jnp.float32)
    w_in = jnp.exp(-rate * (upos + 1.0))[None, :] * first
    w_out = jnp.exp(-rate * (count - 1.0 - upos))[None, :] * final
    diff = upos[:, None] - upos[None, :]
    keep = (diff >= 0.0)[None] & (seg_tok[:, :, None] == seg_tok[:, None, :])
    mask = jnp.where(keep, jnp.exp(-rate * jnp.maximum(diff, 0.0))[None], 0.0)
    bidx = jnp.arange(nblocks, dtype=jnp.int32)
    gap = jnp.maximum(bidx[:, None] - 1 - bidx[None, :], 0).astype(jnp.float32)
    linked = (bidx[None, :] < bidx[:, None]) & (last_seg[None, :] == prev_seg[:, None])
    link = jnp.where(linked, jnp.exp(-rate * count * gap), 0.0)
    return (w_in, w_out, mask, link)

def head_parts(q32, k32, v32, tables):
    w_in, w_out, mask, link = tables
    keys_scaled = (k32 * w_out[..., None]).astype(jnp.bfloat16).astype(jnp.float32)
    states = jnp.einsum('nla,nlb->nab', keys_scaled, v32).astype(jnp.bfloat16)
    incoming = jnp.einsum('ji,iab->jab', link, states.astype(jnp.float32), precision=lax.Precision.HIGHEST).astype(jnp.bfloat16)
    scores = jnp.einsum('nta,nsa->nts', q32, k32)
    weights = (scores * mask).astype(jnp.bfloat16)
    return (weights, incoming)

def head_forward(item, seg_tok, prev_seg, last_seg, count, nblocks):
    qh, kh, vh, rate = item
    q32, k32, v32 = (qh.astype(jnp.float32), kh.astype(jnp.float32), vh.astype(jnp.float32))
    tables = head_tables(rate, seg_tok, prev_seg, last_seg, count, nblocks)
    weights, incoming = head_parts(q32, k32, v32, tables)
    attended = jnp.einsum('nts,nsb->ntb', weights.astype(jnp.float32), v32)
    return attended + tables[0][..., None] * jnp.einsum('nta,nab->ntb', q32, incoming.astype(jnp.float32))

def head_backward(item, seg_tok, prev_seg, last_seg, count, nblocks):
    qh, kh, vh, dh, rate = item
    q32, k32, v32, d32 = (qh.astype(jnp.float32), kh.astype(jnp.float32), vh.astype(jnp.float32), dh.astype(jnp.float32))
    tables = head_tables(rate, seg_tok, prev_seg, last_seg, count, nblocks)
    w_in, w_out, mask, link = tables
    weights, incoming = head_parts(q32, k32, v32, tables)
    weights32 = weights.astype(jnp.float32)
    inc32 = incoming.astype(jnp.float32)
    dweights = (jnp.einsum('ntb,nsb->nts', d32, v32) * mask).astype(jnp.bfloat16).astype(jnp.float32)
    queries_scaled = (q32 * w_in[..., None]).astype(jnp.bfloat16).astype(jnp.float32)
    grads = jnp.einsum('nla,nlb->nab', queries_scaled, d32).astype(jnp.bfloat16)
    outgoing = jnp.einsum('ij,iab->jab', link, grads.astype(jnp.float32), precision=lax.Precision.HIGHEST).astype(jnp.bfloat16).astype(jnp.float32)
    grad_q = jnp.einsum('nts,nsa->nta', dweights, k32) + w_in[..., None] * jnp.einsum('ntb,nab->nta', d32, inc32)
    grad_k = jnp.einsum('nts,nta->nsa', dweights, q32) + w_out[..., None] * jnp.einsum('ntb,nab->nta', v32, outgoing)
    grad_v = jnp.einsum('nts,nta->nsa', weights32, d32) + w_out[..., None] * jnp.einsum('nta,nab->ntb', k32, outgoing)
    return (grad_q, grad_k, grad_v)

def reference(queries, keys, values, doc_lengths, decay_rates, gain, out_grad):
    count = TOK_DEV
    nblocks = N_SEQ
    heads = HEADS
    width = HEAD_SIZE
    tokens, features = queries.shape
    ends = jnp.cumsum(doc_lengths).astype(jnp.int32)
    seg_tok = doc_index(ends, jnp.arange(tokens, dtype=jnp.int32)).reshape(nblocks, count)
    bstart = jnp.arange(nblocks, dtype=jnp.int32) * count
    prev_seg = doc_index(ends, bstart - 1)
    last_seg = doc_index(ends, bstart + count - 1)

    def split(x):
        return x.reshape(nblocks, count, heads, width).transpose(2, 0, 1, 3)

    def merge(x):
        return x.transpose(1, 2, 0, 3).reshape(tokens, features)
    qs, ks, vs = (split(queries), split(keys), split(values))
    outs = lax.map(lambda item: head_forward(item, seg_tok, prev_seg, last_seg, count, nblocks), (qs, ks, vs, decay_rates))
    flat = merge(outs)
    dyf = out_grad.astype(jnp.float32)
    scaled_grad = gain[None, :] * dyf
    inv = lax.rsqrt(lax.optimization_barrier(jnp.sum(flat * flat, axis=1)) / features + EPS)
    dot = lax.optimization_barrier(jnp.sum(scaled_grad * flat, axis=1))
    gain_grad = lax.optimization_barrier(jnp.sum(dyf * flat * inv[:, None], axis=0)) * (1.0 / math.sqrt(tokens))
    dout = (inv[:, None] * scaled_grad - flat * (inv * inv * inv * dot / features)[:, None]).astype(jnp.bfloat16)
    grads = lax.map(lambda item: head_backward(item, seg_tok, prev_seg, last_seg, count, nblocks), (qs, ks, vs, split(dout), decay_rates))
    return (merge(grads[0]).astype(jnp.bfloat16), merge(grads[1]).astype(jnp.bfloat16), merge(grads[2]).astype(jnp.bfloat16), gain_grad)
```

```python
import math

import jax
import jax.numpy as jnp
from jax import lax
from jax.experimental import pallas as pl
from jax.experimental.pallas import tpu as pltpu
from jax.sharding import PartitionSpec as P

EPS = 1e-06
MESH = pl.DeviceIdType.MESH
F32 = jnp.float32
BF16 = jnp.bfloat16
NT = (((1,), (1,)), ((), ()))
TN = (((0,), (0,)), ((), ()))
NN = (((1,), (0,)), ((), ()))

T = 512
HALF = T // 2
W = 128
H = 6
FEATURES = 6144
TOKENS = 16384
SEQ = 32
M = 8
G = SEQ // M
ROWS = W // M
NHEAD = 8
DOCS = 32


def dot(a, b, dims):
    return lax.dot_general(a, b, dims, preferred_element_type=F32)


def kernel(
    docs,
    rates,
    gain,
    q_hbm,
    k_hbm,
    v_hbm,
    og_hbm,
    gq_hbm,
    gk_hbm,
    gv_hbm,
    gg_ref,
    q_s,
    k_s,
    v_s,
    og_s,
    w_s,
    dw_s,
    keep_s,
    att_s,
    d_s,
    qt_s,
    dk_s,
    dv_s,
    gq_s,
    gk_s,
    gv_s,
    share_out,
    share_in,
    tot_out,
    tot_in,
    carry_s,
    loc_s,
    back_out,
    back_in,
    sum_out,
    sum_in,
    gain_mine,
    gain_in,
    gain_tot,
    gain_all,
    in_sem,
    out_sem,
    share_ss,
    share_rs,
    tot_ss,
    tot_rs,
    back_ss,
    back_rs,
    sum_ss,
    sum_rs,
    ga_ss,
    ga_rs,
    gb_ss,
    gb_rs,
):
    s = lax.axis_index("seq")
    hd = lax.axis_index("head")
    g = s // M
    m = lax.rem(s, M)

    def member(i):
        return (g * M + i, hd)

    def peer(k):
        return lax.rem(m + k, M)

    barrier = pltpu.get_barrier_semaphore()
    for k in range(1, M):
        pl.semaphore_signal(barrier, inc=1, device_id=member(peer(k)), device_id_type=MESH)
    for k in range(1, G):
        pl.semaphore_signal(
            barrier, inc=1, device_id=(lax.rem(s + k * M, SEQ), hd), device_id_type=MESH
        )
    for k in range(1, NHEAD):
        pl.semaphore_signal(
            barrier, inc=1, device_id=(s, lax.rem(hd + k, NHEAD)), device_id_type=MESH
        )

    hbm = (k_hbm, v_hbm, q_hbm, og_hbm)
    vmem = (k_s, v_s, q_s, og_s)

    def load(a, h):
        cols = pl.ds(pl.multiple_of(h * W, W), W)
        return pltpu.make_async_copy(hbm[a].at[:, cols], vmem[a].at[h], in_sem.at[a, h])

    for h in range(H):
        load(0, h).start()
        load(1, h).start()
    for h in range(H):
        load(2, h).start()
    for h in range(H):
        load(3, h).start()

    begin = s * T
    far = jnp.int32(1 << 24)
    total = jnp.int32(0)
    bits = jnp.int32(0)
    first_end = far
    last_start = -far
    rel = []
    for d in range(DOCS):
        total = total + docs[d]
        here = total - begin
        rel.append(here)
        if d < DOCS - 1:
            bits = bits | lax.shift_left(jnp.int32(1), lax.shift_right_logical(total, 9))
        first_end = jnp.where((here >= 0) & (first_end == far), here, first_end)
        last_start = jnp.where(here <= T - 1, here, last_start)

    def clear(at, count):
        if count == 0:
            return jnp.float32(1.0)
        field = lax.shift_right_logical(bits, at) & jnp.int32((1 << count) - 1)
        return jnp.where(field == 0, jnp.float32(1.0), jnp.float32(0.0))

    ucol = lax.broadcasted_iota(jnp.int32, (T, W), 0)
    ucol_f = ucol.astype(F32)
    urow_f = lax.broadcasted_iota(jnp.int32, (1, T), 1).astype(F32)

    def w_in_of(r):
        return jnp.where(ucol < first_end, jnp.exp(-r * (ucol_f + 1.0)), 0.0)

    def w_out_of(r):
        return jnp.where(ucol >= last_start, jnp.exp(-r * (T - 1.0 - ucol_f)), 0.0)

    def power(r, n):
        return jnp.exp(jnp.full((1, W), -r * (T * n), F32))

    def mask_of(r, lo, c):
        er = jnp.exp(-r * ucol_f[lo:])
        er = jnp.concatenate([er, er], axis=1)
        ek = jnp.exp(r * urow_f[:, c : c + HALF])
        return er * ek * keep_s[lo:, c : c + HALF]

    for h in range(H):
        load(0, h).wait()
        load(1, h).wait()
        ks = (k_s[h].astype(F32) * w_out_of(rates[h])).astype(BF16)
        st = dot(ks, v_s[h], TN).astype(BF16)
        for i in range(M):
            share_out[0, i, h] = st[i * ROWS : (i + 1) * ROWS]

    pl.semaphore_wait(barrier, M - 1 + G - 1 + NHEAD - 1)

    def share(way, k):
        to = peer(k)
        return pltpu.make_async_remote_copy(
            src_ref=share_out.at[way, to],
            dst_ref=share_in.at[way, m],
            send_sem=share_ss.at[way, k - 1],
            recv_sem=share_rs.at[way, k - 1],
            device_id=member(to),
            device_id_type=MESH,
        )

    def back(way, k):
        to = peer(k)
        return pltpu.make_async_remote_copy(
            src_ref=back_out.at[way, to],
            dst_ref=back_in.at[way, m],
            send_sem=back_ss.at[way, k - 1],
            recv_sem=back_rs.at[way, k - 1],
            device_id=member(to),
            device_id_type=MESH,
        )

    def tot(way, k):
        step = k * M if way == 0 else SEQ - k * M
        return pltpu.make_async_remote_copy(
            src_ref=tot_out.at[way],
            dst_ref=tot_in.at[way, k - 1],
            send_sem=tot_ss.at[way, k - 1],
            recv_sem=tot_rs.at[way, k - 1],
            device_id=(lax.rem(s + step, SEQ), hd),
            device_id_type=MESH,
        )

    def sends(way, k):
        return g + k < G if way == 0 else g - k >= 0

    def receives(way, k):
        return g - k >= 0 if way == 0 else g + k < G

    def start_shares(way):
        for k in range(1, M):
            share(way, k).start()
        share_in[way, m] = share_out[way, m]

    def start_totals(way):
        for k in range(1, M):
            share(way, k).wait_recv()
        one = [power(rates[h], 1.0) for h in range(H)]
        run = [jnp.zeros((ROWS, W), F32) for _ in range(H)]
        for i in range(M) if way == 0 else reversed(range(M)):
            free = clear(g * M + i, 1)
            for h in range(H):
                loc_s[i, h] = run[h]
                run[h] = run[h] * (one[h] * free) + share_in[way, i, h].astype(F32)
        for h in range(H):
            tot_out[way, h] = run[h].astype(BF16)
        for k in range(1, G):

            @pl.when(sends(way, k))
            def _():
                tot(way, k).start()

    def start_back(way):
        near = lax.rem(g + (G - 1 if way == 0 else 1), G)
        next_near = lax.rem(g + (G - 2 if way == 0 else 2), G)
        free1 = clear(near * M, M)
        free2 = free1 * clear(next_near * M, M)
        coef = [
            None,
            [power(rates[h], 1.0 * M) * free1 for h in range(H)],
            [power(rates[h], 2.0 * M) * free2 for h in range(H)],
        ]
        spread = []
        for i in range(M):
            n = i if way == 0 else M - 1 - i
            free = clear(g * M if way == 0 else g * M + i + 1, n)
            spread.append([power(rates[h], 1.0 * n) * free for h in range(H)])
        carry_s[...] = jnp.zeros_like(carry_s)
        for k in range(1, G):

            @pl.when(receives(way, k))
            def _():
                tot(way, k).wait_recv()
                for h in range(H):
                    term = tot_in[way, k - 1, h].astype(F32)
                    if k > 1:
                        term = term * coef[k - 1][h]
                    carry_s[h] = carry_s[h] + term

        for h in range(H):
            carry = carry_s[h]
            for i in range(M):
                back_out[way, i, h] = (loc_s[i, h] + carry * spread[i][h]).astype(BF16)
        for k in range(1, M):
            back(way, k).start()
        back_in[way, m] = back_out[way, m]

    def wait_back(way):
        for k in range(1, M):
            back(way, k).wait_recv()

    def finish(way):
        for k in range(1, M):
            share(way, k).wait_send()
            back(way, k).wait_send()
        for k in range(1, G):

            @pl.when(sends(way, k))
            def _():
                tot(way, k).wait_send()

    def whole(way, h):
        return back_in[way, :, h].reshape(W, W)

    def forward(h, _):
        r = rates[h]
        for c in (0, HALF):
            scores = dot(q_s[h, c:], k_s[h, c : c + HALF], NT)
            w_s[h, c:, c : c + HALF] = (scores * mask_of(r, c, c)).astype(BF16)
        att_s[h, :HALF] = dot(w_s[h, :HALF, :HALF], v_s[h, :HALF], NN)
        att_s[h, HALF:] = dot(w_s[h, HALF:], v_s[h], NN)
        qs = (q_s[h].astype(F32) * w_in_of(r)).astype(BF16)
        qt_s[h] = qs.T
        return 0

    def backward(h, _):
        r = rates[h]
        for c in (0, HALF):
            dw = dot(d_s[h, c:], v_s[h, c : c + HALF], NT)
            dw_s[c:, c : c + HALF] = (dw * mask_of(r, c, c)).astype(BF16)
        far_q = w_in_of(r) * dot(d_s[h], whole(0, h), NT)
        gq_s[h, :HALF] = (
            dot(dw_s[:HALF, :HALF], k_s[h, :HALF], NN) + far_q[:HALF]
        ).astype(BF16)
        gq_s[h, HALF:] = (dot(dw_s[HALF:], k_s[h], NN) + far_q[HALF:]).astype(BF16)
        store(0, h).start()
        dk_s[h, :HALF] = dot(dw_s[:, :HALF], q_s[h], TN)
        dk_s[h, HALF:] = dot(dw_s[HALF:, HALF:], q_s[h, HALF:], TN)
        dv_s[h, :HALF] = dot(w_s[h, :, :HALF], d_s[h], TN)
        dv_s[h, HALF:] = dot(w_s[h, HALF:, HALF:], d_s[h, HALF:], TN)
        return 0

    outs = (gq_hbm, gk_hbm, gv_hbm)
    held = (gq_s, gk_s, gv_s)

    def store(a, h):
        cols = pl.ds(pl.multiple_of(h * W, W), W)
        return pltpu.make_async_copy(held[a].at[h], outs[a].at[:, cols], out_sem.at[a, h])

    start_shares(0)
    start = jnp.full((T, W), -far, jnp.int32)
    for d in range(DOCS):
        start = jnp.where(ucol >= rel[d], rel[d], start)
    for c in range(0, T, W):
        col = lax.broadcasted_iota(jnp.int32, (T, W), 1) + c
        keep_s[:, c : c + W] = jnp.where((col >= start) & (col <= ucol), 1.0, 0.0)
    for h in range(H):
        load(2, h).wait()
    lax.fori_loop(0, 2, forward, 0)
    start_totals(0)
    lax.fori_loop(2, 4, forward, 0)
    start_back(0)
    lax.fori_loop(4, H, forward, 0)
    for h in range(H):
        load(3, h).wait()
    wait_back(0)

    squares = jnp.zeros((T, W), F32)
    dots = jnp.zeros((T, W), F32)
    for h in range(H):
        att = att_s[h] + w_in_of(rates[h]) * dot(q_s[h], whole(0, h), NN)
        att_s[h] = att
        squares = squares + att * att
        dots = dots + gain[:, h * W : (h + 1) * W] * og_s[h].astype(F32) * att

    def halves(x):
        high = x.astype(BF16)
        return [high, (x - high.astype(F32)).astype(BF16)]

    terms = jnp.concatenate(halves(squares) + halves(dots), axis=1)
    row = lax.broadcasted_iota(jnp.int32, (8, 4 * W), 0)
    lane = lax.broadcasted_iota(jnp.int32, (8, 4 * W), 1)
    pick = jnp.where((lane >= 2 * W) == (row == 1), 1.0, 0.0).astype(BF16)
    sums = dot(pick, terms, NT)
    sum_out[...] = sums[:2]

    def head_sum(k):
        return pltpu.make_async_remote_copy(
            src_ref=sum_out,
            dst_ref=sum_in.at[hd],
            send_sem=sum_ss.at[k - 1],
            recv_sem=sum_rs.at[k - 1],
            device_id=(s, lax.rem(hd + k, NHEAD)),
            device_id_type=MESH,
        )

    for k in range(1, NHEAD):
        head_sum(k).start()
    sum_in[hd] = sum_out[...]
    for k in range(1, NHEAD):
        head_sum(k).wait_recv()
    both = sum_in[0]
    for i in range(1, NHEAD):
        both = both + sum_in[i]
    inv = lax.rsqrt(both[0:1] / FEATURES + EPS)
    scale = inv * inv * inv * both[1:2] / FEATURES
    table = jnp.concatenate([inv, scale, jnp.zeros((6, T), F32)], axis=0).T
    inv = jnp.broadcast_to(table[:, 0:1], (T, W))
    scale = jnp.broadcast_to(table[:, 1:2], (T, W))

    for h in range(H):
        grad = gain[:, h * W : (h + 1) * W] * og_s[h].astype(F32)
        d_s[h] = (inv * grad - att_s[h] * scale).astype(BF16)
        gr = dot(qt_s[h], d_s[h], NN).astype(BF16)
        for i in range(M):
            share_out[1, i, h] = gr[i * ROWS : (i + 1) * ROWS]

    start_shares(1)

    for h in range(H):
        term = og_s[h].astype(F32) * att_s[h] * inv
        gain_mine[:, h * W : (h + 1) * W] = jnp.sum(term, axis=0, keepdims=True)

    def gain_a(k):
        return pltpu.make_async_remote_copy(
            src_ref=gain_mine,
            dst_ref=gain_in.at[m],
            send_sem=ga_ss.at[k - 1],
            recv_sem=ga_rs.at[k - 1],
            device_id=member(peer(k)),
            device_id_type=MESH,
        )

    def gain_b(k):
        return pltpu.make_async_remote_copy(
            src_ref=gain_tot,
            dst_ref=gain_all.at[g],
            send_sem=gb_ss.at[k - 1],
            recv_sem=gb_rs.at[k - 1],
            device_id=(lax.rem(s + k * M, SEQ), hd),
            device_id_type=MESH,
        )

    for k in range(1, M):
        gain_a(k).start()
    gain_in[m] = gain_mine[...]

    lax.fori_loop(0, 2, backward, 0)
    start_totals(1)
    for k in range(1, M):
        gain_a(k).wait_recv()
    part = gain_in[0]
    for i in range(1, M):
        part = part + gain_in[i]
    gain_tot[...] = part
    for k in range(1, G):
        gain_b(k).start()
    gain_all[g] = part
    lax.fori_loop(2, 4, backward, 0)
    start_back(1)
    lax.fori_loop(4, H, backward, 0)
    for k in range(1, G):
        gain_b(k).wait_recv()
    part = gain_all[0]
    for i in range(1, G):
        part = part + gain_all[i]
    gg_ref[...] = part * (1.0 / math.sqrt(TOKENS))
    wait_back(1)

    for h in range(H):
        w_out = w_out_of(rates[h])
        out = whole(1, h)
        gk_s[h] = (dk_s[h] + w_out * dot(v_s[h], out, NT)).astype(BF16)
        store(1, h).start()
        gv_s[h] = (dv_s[h] + w_out * dot(k_s[h], out, NN)).astype(BF16)
        store(2, h).start()

    finish(0)
    finish(1)
    for k in range(1, NHEAD):
        head_sum(k).wait_send()
    for k in range(1, M):
        gain_a(k).wait_send()
    for k in range(1, G):
        gain_b(k).wait_send()
    for a in range(3):
        for h in range(H):
            store(a, h).wait()


def on_device(queries, keys, values, doc_lengths, decay_rates, gain, out_grad):
    any_space = pl.BlockSpec(memory_space=pl.ANY)
    smem = pl.BlockSpec(memory_space=pltpu.SMEM)
    vmem = pl.BlockSpec(memory_space=pltpu.VMEM)
    block = jax.ShapeDtypeStruct((T, H * W), BF16)
    dma = pltpu.SemaphoreType.DMA
    wide = pltpu.VMEM((H, T, W), BF16)
    wide32 = pltpu.VMEM((H, T, W), F32)
    shares = pltpu.VMEM((2, M, H, ROWS, W), BF16)
    gq, gk, gv, gg = pl.pallas_call(
        kernel,
        out_shape=(block, block, block, jax.ShapeDtypeStruct((1, H * W), F32)),
        in_specs=[smem, smem, vmem, any_space, any_space, any_space, any_space],
        out_specs=(any_space, any_space, any_space, vmem),
        scratch_shapes=[
            wide,
            wide,
            wide,
            wide,
            pltpu.VMEM((H, T, T), BF16),
            pltpu.VMEM((T, T), BF16),
            pltpu.VMEM((T, T), F32),
            wide32,
            wide,
            pltpu.VMEM((H, W, T), BF16),
            wide32,
            wide32,
            wide,
            wide,
            wide,
            shares,
            shares,
            pltpu.VMEM((2, H, ROWS, W), BF16),
            pltpu.VMEM((2, G - 1, H, ROWS, W), BF16),
            pltpu.VMEM((H, ROWS, W), F32),
            pltpu.VMEM((M, H, ROWS, W), F32),
            shares,
            shares,
            pltpu.VMEM((2, T), F32),
            pltpu.VMEM((NHEAD, 2, T), F32),
            pltpu.VMEM((1, H * W), F32),
            pltpu.VMEM((M, 1, H * W), F32),
            pltpu.VMEM((1, H * W), F32),
            pltpu.VMEM((G, 1, H * W), F32),
            dma((4, H)),
            dma((3, H)),
            dma((2, M - 1)),
            dma((2, M - 1)),
            dma((2, G - 1)),
            dma((2, G - 1)),
            dma((2, M - 1)),
            dma((2, M - 1)),
            dma((NHEAD - 1,)),
            dma((NHEAD - 1,)),
            dma((M - 1,)),
            dma((M - 1,)),
            dma((G - 1,)),
            dma((G - 1,)),
        ],
        compiler_params=pltpu.CompilerParams(
            collective_id=0, has_side_effects=True, vmem_limit_bytes=48 << 20
        ),
        cost_estimate=pl.CostEstimate(
            flops=2 * H * (6 * T * T * W + 6 * T * W * W),
            bytes_accessed=7 * T * H * W * 2,
            transcendentals=4 * H * T * W,
        ),
    )(doc_lengths, decay_rates, gain.reshape(1, H * W), queries, keys, values, out_grad)
    return gq, gk, gv, gg.reshape(H * W)


def solution(mesh):
    return jax.shard_map(
        on_device,
        mesh=mesh,
        in_specs=(
            P("seq", "head"),
            P("seq", "head"),
            P("seq", "head"),
            P(),
            P("head"),
            P("head"),
            P("seq", "head"),
        ),
        out_specs=(P("seq", "head"), P("seq", "head"), P("seq", "head"), P("head")),
        check_vma=False,
    )
```

```python
import math

import jax
import jax.numpy as jnp
from jax import lax
from jax.experimental import pallas as pl
from jax.experimental.pallas import tpu as pltpu
from jax.sharding import PartitionSpec as P

EPS = 1e-06
MESH = pl.DeviceIdType.MESH
F32 = jnp.float32
BF16 = jnp.bfloat16
NT = (((1,), (1,)), ((), ()))
TN = (((0,), (0,)), ((), ()))
NN = (((1,), (0,)), ((), ()))

T = 512
HALF = T // 2
W = 128
H = 6
FEATURES = 6144
TOKENS = 16384
SEQ = 32
M = 8
G = SEQ // M
NX = 4
OFFSETS = ((1, 2), (1, 1), (1, 3), (1, 0), (0, 2), (0, 1), (0, 3))
FAR_FIRST = (2, 3, 1)
PARTS = 2
HB = H // PARTS
ROWS = W // M
NHEAD = 8
DOCS = 32


def dot(a, b, dims):
    return lax.dot_general(a, b, dims, preferred_element_type=F32)


def kernel(
    docs,
    rates,
    gain,
    q_hbm,
    k_hbm,
    v_hbm,
    og_hbm,
    gq_s,
    gk_s,
    gv_s,
    gg_ref,
    q_s,
    k_s,
    v_s,
    og_s,
    w_s,
    dw_s,
    keep_s,
    wi_s,
    wo_s,
    g_s,
    dk_s,
    dv_s,
    att_s,
    d_s,
    qt_s,
    inc_s,
    squares_s,
    dots_s,
    one_s,
    coef_s,
    spread_s,
    share_out,
    share_in,
    tot_out,
    tot_in,
    carry_s,
    loc_s,
    back_out,
    back_in,
    sum_out,
    sum_in,
    gain_mine,
    gain_in,
    gain_tot,
    gain_all,
    in_sem,
    share_ss,
    share_rs,
    tot_ss,
    tot_rs,
    back_ss,
    back_rs,
    sum_ss,
    sum_rs,
    ga_ss,
    ga_rs,
    gb_ss,
    gb_rs,
):
    s = lax.axis_index("seq")
    hd = lax.axis_index("head")
    g = s // M
    m = lax.rem(s, M)

    def member(i):
        return (g * M + i, hd)

    def peer(o):
        dz, dx = OFFSETS[o]
        return lax.rem(m // NX + dz, 2) * NX + lax.rem(lax.rem(m, NX) + dx, NX)

    def place(group, i):
        return lax.rem(i + jnp.where(group >= G // 2, NX, 0), M)

    mine = place(g, m)

    def ally(k):
        other = lax.rem(g + k, G)
        return (other * M + place(other, mine), hd)

    barrier = pltpu.get_barrier_semaphore()
    for o in range(M - 1):
        pl.semaphore_signal(barrier, inc=1, device_id=member(peer(o)), device_id_type=MESH)
    for k in range(1, G):
        pl.semaphore_signal(barrier, inc=1, device_id=ally(k), device_id_type=MESH)
    for k in range(1, NHEAD):
        pl.semaphore_signal(
            barrier, inc=1, device_id=(s, lax.rem(hd + k, NHEAD)), device_id_type=MESH
        )

    hbm = (k_hbm, v_hbm, q_hbm, og_hbm)
    vmem = (k_s, v_s, q_s, og_s)

    def load(a, h):
        return pltpu.make_async_copy(
            hbm[a].at[:, h * W : (h + 1) * W], vmem[a].at[h], in_sem.at[a, h]
        )

    for h in range(H):
        load(0, h).start()
        load(1, h).start()
    for h in range(H):
        load(2, h).start()
        load(3, h).start()

    begin = s * T
    far = jnp.int32(1 << 24)
    total = jnp.int32(0)
    bits = jnp.int32(0)
    first_end = far
    last_start = -far
    rel = []
    for d in range(DOCS):
        total = total + docs[d]
        here = total - begin
        rel.append(here)
        if d < DOCS - 1:
            bits = bits | lax.shift_left(jnp.int32(1), lax.shift_right_logical(total, 9))
        first_end = jnp.where((here >= 0) & (first_end == far), here, first_end)
        last_start = jnp.where(here <= T - 1, here, last_start)

    def clear(at, count):
        if count == 0:
            return jnp.float32(1.0)
        field = lax.shift_right_logical(bits, at) & jnp.int32((1 << count) - 1)
        return jnp.where(field == 0, jnp.float32(1.0), jnp.float32(0.0))

    ucol = lax.broadcasted_iota(jnp.int32, (T, W), 0)
    ucol_f = ucol.astype(F32)
    urow_f = lax.broadcasted_iota(jnp.int32, (1, T), 1).astype(F32)

    def mask_of(r, lo, c):
        er = jnp.exp(-r * ucol_f[lo:])
        er = jnp.concatenate([er, er], axis=1)
        ek = jnp.exp(r * urow_f[:, c : c + HALF])
        return er * ek * keep_s[lo:, c : c + HALF]

    def share(way, b, o):
        to = peer(o)
        return pltpu.make_async_remote_copy(
            src_ref=share_out.at[way, b, place(g, to)],
            dst_ref=share_in.at[way, b, m],
            send_sem=share_ss.at[way, b, o],
            recv_sem=share_rs.at[way, b, o],
            device_id=member(to),
            device_id_type=MESH,
        )

    def back(way, b, o):
        to = peer(o)
        return pltpu.make_async_remote_copy(
            src_ref=back_out.at[way, b, to],
            dst_ref=back_in.at[way, b, mine],
            send_sem=back_ss.at[way, b, o],
            recv_sem=back_rs.at[way, b, o],
            device_id=member(to),
            device_id_type=MESH,
        )

    def tot(way, b, k):
        return pltpu.make_async_remote_copy(
            src_ref=tot_out.at[way, b],
            dst_ref=tot_in.at[way, b, k - 1],
            send_sem=tot_ss.at[way, b, k - 1],
            recv_sem=tot_rs.at[way, b, k - 1],
            device_id=ally(k if way == 0 else G - k),
            device_id_type=MESH,
        )

    def sends(way, k):
        return g + k < G if way == 0 else g - k >= 0

    def receives(way, k):
        return g - k >= 0 if way == 0 else g + k < G

    def start_shares(way, b):
        for o in range(M - 1):
            share(way, b, o).start()
        share_in[way, b, m] = share_out[way, b, mine]

    def start_totals(way, b):
        for o in reversed(range(M - 1)):
            share(way, b, o).wait_recv()
        run = [jnp.zeros((ROWS, W), F32) for _ in range(HB)]
        for i in range(M) if way == 0 else reversed(range(M)):
            for e in range(HB):
                h = b * HB + e
                loc_s[b, i, e] = run[e]
                run[e] = run[e] * one_s[i, h : h + 1] + share_in[way, b, i, e].astype(F32)
        for e in range(HB):
            tot_out[way, b, e] = run[e].astype(BF16)
        for k in FAR_FIRST:

            @pl.when(sends(way, k))
            def _():
                tot(way, b, k).start()

    def start_back(way, b):
        carry_s[b] = jnp.zeros((HB, ROWS, W), F32)
        for k in reversed(FAR_FIRST):

            @pl.when(receives(way, k))
            def _():
                tot(way, b, k).wait_recv()
                for e in range(HB):
                    h = b * HB + e
                    term = tot_in[way, b, k - 1, e].astype(F32)
                    if k > 1:
                        term = term * coef_s[way, k - 2, h : h + 1]
                    carry_s[b, e] = carry_s[b, e] + term

        for e in range(HB):
            h = b * HB + e
            carry = carry_s[b, e]
            for i in range(M):
                back_out[way, b, i, e] = (
                    loc_s[b, i, e] + carry * spread_s[way, i, h : h + 1]
                ).astype(BF16)
        for o in range(M - 1):
            back(way, b, o).start()
        back_in[way, b, mine] = back_out[way, b, m]

    def wait_back(way, b):
        for o in reversed(range(M - 1)):
            back(way, b, o).wait_recv()

    def whole(way, b, e):
        return back_in[way, b, :, e].reshape(W, W)

    def forward(h, _):
        r = rates[h]
        for c in (0, HALF):
            scores = dot(q_s[h, c:], k_s[h, c : c + HALF], NT)
            w_s[h, c:, c : c + HALF] = (scores * mask_of(r, c, c)).astype(BF16)
        att_s[h, :HALF] = dot(w_s[h, :HALF, :HALF], v_s[h, :HALF], NN)
        att_s[h, HALF:] = dot(w_s[h, HALF:], v_s[h], NN)
        w_in = jnp.where(ucol < first_end, jnp.exp(-r * (ucol_f + 1.0)), 0.0)
        wi_s[h] = w_in
        qt_s[h] = (q_s[h].astype(F32) * w_in).astype(BF16).T
        return 0

    def backward(h, _):
        r = rates[h]
        for c in (0, HALF):
            dw = dot(d_s[h, c:], v_s[h, c : c + HALF], NT)
            dw_s[c:, c : c + HALF] = (dw * mask_of(r, c, c)).astype(BF16)
        far_q = wi_s[h] * dot(d_s[h], inc_s[h], NT)
        cols = pl.ds(pl.multiple_of(h * W, W), W)
        gq_s[:HALF, cols] = (
            dot(dw_s[:HALF, :HALF], k_s[h, :HALF], NN) + far_q[:HALF]
        ).astype(BF16)
        gq_s[HALF:, cols] = (dot(dw_s[HALF:], k_s[h], NN) + far_q[HALF:]).astype(BF16)
        dk_s[h, :HALF] = dot(dw_s[:, :HALF], q_s[h], TN)
        dk_s[h, HALF:] = dot(dw_s[HALF:, HALF:], q_s[h, HALF:], TN)
        dv_s[h, :HALF] = dot(w_s[h, :, :HALF], d_s[h], TN)
        dv_s[h, HALF:] = dot(w_s[h, HALF:, HALF:], d_s[h, HALF:], TN)
        return 0

    for b in range(PARTS):
        for e in range(HB):
            h = b * HB + e
            load(0, h).wait()
            load(1, h).wait()
            w_out = jnp.where(
                ucol >= last_start, jnp.exp(-rates[h] * (T - 1.0 - ucol_f)), 0.0
            )
            wo_s[h] = w_out
            ks = (k_s[h].astype(F32) * w_out).astype(BF16)
            st = dot(ks, v_s[h], TN).astype(BF16)
            for i in range(M):
                share_out[0, b, i, e] = st[i * ROWS : (i + 1) * ROWS]
        if b == 0:
            pl.semaphore_wait(barrier, M - 1 + G - 1 + NHEAD - 1)
        start_shares(0, b)

    row = lax.broadcasted_iota(jnp.int32, (8, W), 0)
    rate_rows = jnp.zeros((8, W), F32)
    for h in range(H):
        rate_rows = jnp.where(row == h, rates[h], rate_rows)

    def power(n):
        return jnp.exp(rate_rows * (-float(T) * n))

    for i in range(M):
        one_s[i] = power(1) * clear(g * M + i, 1)
        spread_s[0, i] = power(i) * clear(g * M, i)
        spread_s[1, i] = power(M - 1 - i) * clear(g * M + i + 1, M - 1 - i)
    for way in range(2):
        near = lax.rem(g + (G - 1 if way == 0 else 1), G)
        next_near = lax.rem(g + (G - 2 if way == 0 else 2), G)
        free = clear(near * M, M)
        coef_s[way, 0] = power(M) * free
        coef_s[way, 1] = power(2 * M) * (free * clear(next_near * M, M))

    start = jnp.full((T, W), -far, jnp.int32)
    for d in range(DOCS):
        start = jnp.where(ucol >= rel[d], rel[d], start)
    for c in range(0, T, W):
        col = lax.broadcasted_iota(jnp.int32, (T, W), 1) + c
        keep_s[:, c : c + W] = jnp.where((col >= start) & (col <= ucol), 1.0, 0.0)
    for h in range(H):
        load(2, h).wait()
        load(3, h).wait()
        g_s[h] = gain[:, h * W : (h + 1) * W] * og_s[h].astype(F32)
    lax.fori_loop(0, 3, forward, 0)
    for b in range(PARTS):
        start_totals(0, b)
    lax.fori_loop(3, H, forward, 0)
    for b in range(PARTS):
        start_back(0, b)

    squares_s[...] = jnp.zeros_like(squares_s)
    dots_s[...] = jnp.zeros_like(dots_s)
    for b in range(PARTS):
        wait_back(0, b)
        for e in range(HB):
            h = b * HB + e
            inc = whole(0, b, e)
            inc_s[h] = inc
            att = att_s[h] + wi_s[h] * dot(q_s[h], inc, NN)
            att_s[h] = att
            squares_s[...] += att * att
            dots_s[...] += g_s[h] * att

    def halves(x):
        high = x.astype(BF16)
        return [high, (x - high.astype(F32)).astype(BF16)]

    terms = jnp.concatenate(halves(squares_s[...]) + halves(dots_s[...]), axis=1)
    row = lax.broadcasted_iota(jnp.int32, (8, 4 * W), 0)
    lane = lax.broadcasted_iota(jnp.int32, (8, 4 * W), 1)
    pick = jnp.where((lane >= 2 * W) == (row == 1), 1.0, 0.0).astype(BF16)
    sums = dot(pick, terms, NT)
    sum_out[...] = sums[:2]

    def head_sum(k):
        return pltpu.make_async_remote_copy(
            src_ref=sum_out,
            dst_ref=sum_in.at[hd],
            send_sem=sum_ss.at[k - 1],
            recv_sem=sum_rs.at[k - 1],
            device_id=(s, lax.rem(hd + k, NHEAD)),
            device_id_type=MESH,
        )

    for k in range(1, NHEAD):
        head_sum(k).start()
    sum_in[hd] = sum_out[...]
    for k in range(1, NHEAD):
        head_sum(k).wait_recv()
    both = sum_in[0]
    for i in range(1, NHEAD):
        both = both + sum_in[i]
    inv = lax.rsqrt(both[0:1] / FEATURES + EPS)
    scale = inv * inv * inv * both[1:2] / FEATURES
    table = jnp.concatenate([inv, scale, jnp.zeros((6, T), F32)], axis=0).T
    inv = jnp.broadcast_to(table[:, 0:1], (T, W))
    scale = jnp.broadcast_to(table[:, 1:2], (T, W))

    for b in range(PARTS):
        for e in range(HB):
            h = b * HB + e
            d_s[h] = (inv * g_s[h] - att_s[h] * scale).astype(BF16)
            gr = dot(qt_s[h], d_s[h], NN).astype(BF16)
            for i in range(M):
                share_out[1, b, i, e] = gr[i * ROWS : (i + 1) * ROWS]
        start_shares(1, b)

    for h in range(H):
        term = og_s[h].astype(F32) * att_s[h] * inv
        gain_mine[:, h * W : (h + 1) * W] = jnp.sum(term, axis=0, keepdims=True)

    def gain_a(o):
        return pltpu.make_async_remote_copy(
            src_ref=gain_mine,
            dst_ref=gain_in.at[m],
            send_sem=ga_ss.at[o],
            recv_sem=ga_rs.at[o],
            device_id=member(peer(o)),
            device_id_type=MESH,
        )

    def gain_b(k):
        return pltpu.make_async_remote_copy(
            src_ref=gain_tot,
            dst_ref=gain_all.at[g],
            send_sem=gb_ss.at[k - 1],
            recv_sem=gb_rs.at[k - 1],
            device_id=ally(k),
            device_id_type=MESH,
        )

    for o in range(M - 1):
        gain_a(o).start()
    gain_in[m] = gain_mine[...]

    lax.fori_loop(0, 3, backward, 0)
    for b in range(PARTS):
        start_totals(1, b)
    for o in range(M - 1):
        gain_a(o).wait_recv()
    part = gain_in[0]
    for i in range(1, M):
        part = part + gain_in[i]
    gain_tot[...] = part
    for k in range(1, G):
        gain_b(k).start()
    gain_all[g] = part
    lax.fori_loop(3, H, backward, 0)
    for b in range(PARTS):
        start_back(1, b)
    for k in range(1, G):
        gain_b(k).wait_recv()
    part = gain_all[0]
    for i in range(1, G):
        part = part + gain_all[i]
    gg_ref[...] = part * (1.0 / math.sqrt(TOKENS))

    for b in range(PARTS):
        for o in range(M - 1):
            share(0, b, o).wait_send()
            back(0, b, o).wait_send()
            share(1, b, o).wait_send()
        for k in range(1, G):
            for way in range(2):

                @pl.when(sends(way, k))
                def _():
                    tot(way, b, k).wait_send()

    for k in range(1, NHEAD):
        head_sum(k).wait_send()
    for o in range(M - 1):
        gain_a(o).wait_send()
    for k in range(1, G):
        gain_b(k).wait_send()

    for b in range(PARTS):
        wait_back(1, b)
        for e in range(HB):
            h = b * HB + e
            out = whole(1, b, e)
            gk_s[:, h * W : (h + 1) * W] = (dk_s[h] + wo_s[h] * dot(v_s[h], out, NT)).astype(BF16)
            gv_s[:, h * W : (h + 1) * W] = (dv_s[h] + wo_s[h] * dot(k_s[h], out, NN)).astype(BF16)
    for b in range(PARTS):
        for o in range(M - 1):
            back(1, b, o).wait_send()


def write(gq_s, gk_s, gv_s, gg_s, gq_hbm, gk_hbm, gv_hbm, gg_ref, sem):
    held = (gq_s, gk_s, gv_s)
    outs = (gq_hbm, gk_hbm, gv_hbm)

    def store(a, c):
        rows = slice(c * W, (c + 1) * W)
        return pltpu.make_async_copy(held[a].at[rows], outs[a].at[rows], sem.at[a, c])

    for a in range(3):
        for c in range(T // W):
            store(a, c).start()
    for h in range(H):
        gg_ref[h * W : (h + 1) * W] = gg_s[0, h * W : (h + 1) * W]
    for a in range(3):
        for c in range(T // W):
            store(a, c).wait()


def on_device(queries, keys, values, doc_lengths, decay_rates, gain, out_grad):
    hbm = pl.BlockSpec(memory_space=pltpu.HBM)
    smem = pl.BlockSpec(memory_space=pltpu.SMEM)
    vmem = pl.BlockSpec(memory_space=pltpu.VMEM)
    dma = pltpu.SemaphoreType.DMA
    wide = (H, T, W)
    shares = pltpu.VMEM((2, PARTS, M, HB, ROWS, W), BF16)
    block = jax.ShapeDtypeStruct((T, H * W), BF16)
    row = jax.ShapeDtypeStruct((1, H * W), F32)
    gq, gk, gv, gg = pl.pallas_call(
        kernel,
        out_shape=(
            block,
            block,
            block,
            row,
        ),
        in_specs=[smem, smem, vmem, hbm, hbm, hbm, hbm],
        out_specs=(vmem,) * 4,
        scratch_shapes=[
            pltpu.VMEM(wide, BF16),
            pltpu.VMEM(wide, BF16),
            pltpu.VMEM(wide, BF16),
            pltpu.VMEM(wide, BF16),
            pltpu.VMEM((H, T, T), BF16),
            pltpu.VMEM((T, T), BF16),
            pltpu.VMEM((T, T), F32),
            pltpu.VMEM(wide, F32),
            pltpu.VMEM(wide, F32),
            pltpu.VMEM(wide, F32),
            pltpu.VMEM(wide, F32),
            pltpu.VMEM(wide, F32),
            pltpu.VMEM(wide, F32),
            pltpu.VMEM(wide, BF16),
            pltpu.VMEM((H, W, T), BF16),
            pltpu.VMEM((H, W, W), BF16),
            pltpu.VMEM((T, W), F32),
            pltpu.VMEM((T, W), F32),
            pltpu.VMEM((M, 8, W), F32),
            pltpu.VMEM((2, 2, 8, W), F32),
            pltpu.VMEM((2, M, 8, W), F32),
            shares,
            shares,
            pltpu.VMEM((2, PARTS, HB, ROWS, W), BF16),
            pltpu.VMEM((2, PARTS, G - 1, HB, ROWS, W), BF16),
            pltpu.VMEM((PARTS, HB, ROWS, W), F32),
            pltpu.VMEM((PARTS, M, HB, ROWS, W), F32),
            shares,
            shares,
            pltpu.VMEM((2, T), F32),
            pltpu.VMEM((NHEAD, 2, T), F32),
            pltpu.VMEM((1, H * W), F32),
            pltpu.VMEM((M, 1, H * W), F32),
            pltpu.VMEM((1, H * W), F32),
            pltpu.VMEM((G, 1, H * W), F32),
            dma((4, H)),
            dma((2, PARTS, M - 1)),
            dma((2, PARTS, M - 1)),
            dma((2, PARTS, G - 1)),
            dma((2, PARTS, G - 1)),
            dma((2, PARTS, M - 1)),
            dma((2, PARTS, M - 1)),
            dma((NHEAD - 1,)),
            dma((NHEAD - 1,)),
            dma((M - 1,)),
            dma((M - 1,)),
            dma((G - 1,)),
            dma((G - 1,)),
        ],
        compiler_params=pltpu.CompilerParams(
            collective_id=0, has_side_effects=True, vmem_limit_bytes=51 << 20
        ),
        cost_estimate=pl.CostEstimate(
            flops=2 * H * (6 * T * T * W + 5 * T * W * W),
            bytes_accessed=4 * T * H * W * 2,
            transcendentals=4 * H * T * W,
        ),
    )(doc_lengths, decay_rates, gain.reshape(1, H * W), queries, keys, values, out_grad)
    gq, gk, gv, gg = pl.pallas_call(
        write,
        out_shape=(block, block, block, jax.ShapeDtypeStruct((H * W,), F32)),
        in_specs=[vmem] * 4,
        out_specs=(hbm, hbm, hbm, vmem),
        scratch_shapes=[dma((3, T // W))],
        compiler_params=pltpu.CompilerParams(vmem_limit_bytes=51 << 20),
        cost_estimate=pl.CostEstimate(
            flops=0, bytes_accessed=3 * T * H * W * 2, transcendentals=0
        ),
    )(gq, gk, gv, gg)
    return gq, gk, gv, gg


def solution(mesh):
    return jax.shard_map(
        on_device,
        mesh=mesh,
        in_specs=(
            P("seq", "head"),
            P("seq", "head"),
            P("seq", "head"),
            P(),
            P("head"),
            P("head"),
            P("seq", "head"),
        ),
        out_specs=(P("seq", "head"), P("seq", "head"), P("seq", "head"), P("head")),
        check_vma=False,
    )
```

```python
import math

import jax
import jax.numpy as jnp
from jax import lax
from jax.experimental import pallas as pl
from jax.experimental.pallas import tpu as pltpu
from jax.sharding import PartitionSpec as P

EPS = 1e-06
MESH = pl.DeviceIdType.MESH
F32 = jnp.float32
BF16 = jnp.bfloat16
NT = (((1,), (1,)), ((), ()))
TN = (((0,), (0,)), ((), ()))
NN = (((1,), (0,)), ((), ()))

T = 512
HALF = T // 2
W = 128
H = 6
FEATURES = 6144
TOKENS = 16384
SEQ = 32
M = 8
G = SEQ // M
NX = 4
OFFSETS = ((1, 2), (1, 1), (1, 3), (1, 0), (0, 2), (0, 1), (0, 3))
FAR_FIRST = (2, 3, 1)
OUT_PARTS = (((0, 4), (4, 6)), ((0, 4), (4, 6)))
BACK_PARTS = (((0, 4), (4, 6)), ((0, 4), (4, 6)))
PARTS = 2
ROWS = W // M
NHEAD = 8
DOCS = 32


def dot(a, b, dims):
    return lax.dot_general(a, b, dims, preferred_element_type=F32)


def kernel(
    docs_hbm,
    rates_hbm,
    gain_hbm,
    q_hbm,
    k_hbm,
    v_hbm,
    og_hbm,
    gq_s,
    gk_s,
    gv_s,
    gg_ref,
    q_s,
    k_s,
    v_s,
    og_s,
    w_s,
    dw_s,
    keep_s,
    wi_s,
    wo_s,
    g_s,
    dk_s,
    dv_s,
    att_s,
    d_s,
    qt_s,
    inc_s,
    squares_s,
    dots_s,
    one_s,
    coef_s,
    spread_s,
    share_out,
    share_in,
    tot_out,
    tot_in,
    carry_s,
    loc_s,
    back_out,
    back_in,
    sum_out,
    sum_in,
    gain_mine,
    gain_in,
    gain_tot,
    gain_all,
    docs,
    rates,
    gain,
    small_sem,
    in_sem,
    share_ss,
    share_rs,
    tot_ss,
    tot_rs,
    back_ss,
    back_rs,
    sum_ss,
    sum_rs,
    ga_ss,
    ga_rs,
    gb_ss,
    gb_rs,
):
    s = lax.axis_index("seq")
    hd = lax.axis_index("head")
    g = s // M
    m = lax.rem(s, M)

    def member(i):
        return (g * M + i, hd)

    def peer(o):
        dz, dx = OFFSETS[o]
        return lax.rem(m // NX + dz, 2) * NX + lax.rem(lax.rem(m, NX) + dx, NX)

    def place(group, i):
        return lax.rem(i + jnp.where(group >= G // 2, NX, 0), M)

    mine = place(g, m)

    def ally(k):
        other = lax.rem(g + k, G)
        return (other * M + place(other, mine), hd)

    barrier = pltpu.get_barrier_semaphore()
    for o in range(M - 1):
        pl.semaphore_signal(barrier, inc=1, device_id=member(peer(o)), device_id_type=MESH)
    for k in range(1, G):
        pl.semaphore_signal(barrier, inc=1, device_id=ally(k), device_id_type=MESH)
    for k in range(1, NHEAD):
        pl.semaphore_signal(
            barrier, inc=1, device_id=(s, lax.rem(hd + k, NHEAD)), device_id_type=MESH
        )

    hbm = (k_hbm, v_hbm, q_hbm, og_hbm)
    vmem = (k_s, v_s, q_s, og_s)

    def load(a, h):
        return pltpu.make_async_copy(
            hbm[a].at[:, h * W : (h + 1) * W], vmem[a].at[h], in_sem.at[a, h]
        )

    small = [
        pltpu.make_async_copy(src, dst, small_sem.at[i])
        for i, (src, dst) in enumerate(((docs_hbm, docs), (rates_hbm, rates), (gain_hbm, gain)))
    ]
    for copy in small:
        copy.start()
    for h in range(H):
        load(0, h).start()
        load(1, h).start()
    for h in range(H):
        load(2, h).start()
        load(3, h).start()

    for copy in small:
        copy.wait()
    begin = s * T
    far = jnp.int32(1 << 24)
    total = jnp.int32(0)
    bits = jnp.int32(0)
    first_end = far
    last_start = -far
    rel = []
    for d in range(DOCS):
        total = total + docs[d]
        here = total - begin
        rel.append(here)
        if d < DOCS - 1:
            bits = bits | lax.shift_left(jnp.int32(1), lax.shift_right_logical(total, 9))
        first_end = jnp.where((here >= 0) & (first_end == far), here, first_end)
        last_start = jnp.where(here <= T - 1, here, last_start)

    def clear(at, count):
        if count == 0:
            return jnp.float32(1.0)
        field = lax.shift_right_logical(bits, at) & jnp.int32((1 << count) - 1)
        return jnp.where(field == 0, jnp.float32(1.0), jnp.float32(0.0))

    ucol = lax.broadcasted_iota(jnp.int32, (T, W), 0)
    ucol_f = ucol.astype(F32)
    urow_f = lax.broadcasted_iota(jnp.int32, (1, T), 1).astype(F32)

    def mask_of(r, lo, c):
        er = jnp.exp(-r * ucol_f[lo:])
        er = jnp.concatenate([er, er], axis=1)
        ek = jnp.exp(r * urow_f[:, c : c + HALF])
        return er * ek * keep_s[lo:, c : c + HALF]

    def share(way, b, o):
        to = peer(o)
        heads = slice(*OUT_PARTS[way][b])
        return pltpu.make_async_remote_copy(
            src_ref=share_out.at[way, place(g, to), heads],
            dst_ref=share_in.at[way, m, heads],
            send_sem=share_ss.at[way, b, o],
            recv_sem=share_rs.at[way, b, o],
            device_id=member(to),
            device_id_type=MESH,
        )

    def back(way, b, o):
        to = peer(o)
        heads = slice(*BACK_PARTS[way][b])
        return pltpu.make_async_remote_copy(
            src_ref=back_out.at[way, to, heads],
            dst_ref=back_in.at[way, mine, heads],
            send_sem=back_ss.at[way, b, o],
            recv_sem=back_rs.at[way, b, o],
            device_id=member(to),
            device_id_type=MESH,
        )

    def tot(way, b, k):
        heads = slice(*OUT_PARTS[way][b])
        return pltpu.make_async_remote_copy(
            src_ref=tot_out.at[way, heads],
            dst_ref=tot_in.at[way, k - 1, heads],
            send_sem=tot_ss.at[way, b, k - 1],
            recv_sem=tot_rs.at[way, b, k - 1],
            device_id=ally(k if way == 0 else G - k),
            device_id_type=MESH,
        )

    def sends(way, k):
        return g + k < G if way == 0 else g - k >= 0

    def receives(way, k):
        return g - k >= 0 if way == 0 else g + k < G

    def start_shares(way, b):
        for o in range(M - 1):
            share(way, b, o).start()
        for h in range(*OUT_PARTS[way][b]):
            share_in[way, m, h] = share_out[way, mine, h]

    def start_totals(way, b):
        for o in reversed(range(M - 1)):
            share(way, b, o).wait_recv()
        for h in range(*OUT_PARTS[way][b]):
            run = jnp.zeros((ROWS, W), F32)
            for i in range(M) if way == 0 else reversed(range(M)):
                loc_s[i, h] = run
                run = run * one_s[i, h : h + 1] + share_in[way, i, h].astype(F32)
            tot_out[way, h] = run.astype(BF16)
        for k in FAR_FIRST:

            @pl.when(sends(way, k))
            def _():
                tot(way, b, k).start()

    def gather_carry(way, b):
        for h in range(*OUT_PARTS[way][b]):
            carry_s[h] = jnp.zeros((ROWS, W), F32)
        for k in reversed(FAR_FIRST):

            @pl.when(receives(way, k))
            def _():
                tot(way, b, k).wait_recv()
                for h in range(*OUT_PARTS[way][b]):
                    term = tot_in[way, k - 1, h].astype(F32)
                    if k > 1:
                        term = term * coef_s[way, k - 2, h : h + 1]
                    carry_s[h] = carry_s[h] + term

    def start_back(way):
        ready = 0
        for b, (lo, hi) in enumerate(BACK_PARTS[way]):
            while ready < len(OUT_PARTS[way]) and OUT_PARTS[way][ready][0] < hi:
                gather_carry(way, ready)
                ready += 1
            for h in range(lo, hi):
                carry = carry_s[h]
                for i in range(M):
                    back_out[way, i, h] = (
                        loc_s[i, h] + carry * spread_s[way, i, h : h + 1]
                    ).astype(BF16)
            for o in range(M - 1):
                back(way, b, o).start()
            for h in range(lo, hi):
                back_in[way, mine, h] = back_out[way, m, h]

    def wait_back(way, b):
        for o in reversed(range(M - 1)):
            back(way, b, o).wait_recv()

    def whole(way, h):
        return back_in[way, :, h].reshape(W, W)

    def forward(h, _):
        r = rates[h]
        for c in (0, HALF):
            scores = dot(q_s[h, c:], k_s[h, c : c + HALF], NT)
            w_s[h, c:, c : c + HALF] = (scores * mask_of(r, c, c)).astype(BF16)
        att_s[h, :HALF] = dot(w_s[h, :HALF, :HALF], v_s[h, :HALF], NN)
        att_s[h, HALF:] = dot(w_s[h, HALF:], v_s[h], NN)
        w_in = jnp.where(ucol < first_end, jnp.exp(-r * (ucol_f + 1.0)), 0.0)
        wi_s[h] = w_in
        qt_s[h] = (q_s[h].astype(F32) * w_in).astype(BF16).T
        return 0

    def backward(h, _):
        r = rates[h]
        for c in (0, HALF):
            dw = dot(d_s[h, c:], v_s[h, c : c + HALF], NT)
            dw_s[c:, c : c + HALF] = (dw * mask_of(r, c, c)).astype(BF16)
        far_q = wi_s[h] * dot(d_s[h], inc_s[h], NT)
        cols = pl.ds(pl.multiple_of(h * W, W), W)
        gq_s[:HALF, cols] = (
            dot(dw_s[:HALF, :HALF], k_s[h, :HALF], NN) + far_q[:HALF]
        ).astype(BF16)
        gq_s[HALF:, cols] = (dot(dw_s[HALF:], k_s[h], NN) + far_q[HALF:]).astype(BF16)
        dk_s[h, :HALF] = dot(dw_s[:, :HALF], q_s[h], TN)
        dk_s[h, HALF:] = dot(dw_s[HALF:, HALF:], q_s[h, HALF:], TN)
        dv_s[h, :HALF] = dot(w_s[h, :, :HALF], d_s[h], TN)
        dv_s[h, HALF:] = dot(w_s[h, HALF:, HALF:], d_s[h, HALF:], TN)
        return 0

    for b, (lo, hi) in enumerate(OUT_PARTS[0]):
        for h in range(lo, hi):
            load(0, h).wait()
            load(1, h).wait()
            w_out = jnp.where(
                ucol >= last_start, jnp.exp(-rates[h] * (T - 1.0 - ucol_f)), 0.0
            )
            wo_s[h] = w_out
            ks = (k_s[h].astype(F32) * w_out).astype(BF16)
            st = dot(ks, v_s[h], TN).astype(BF16)
            for i in range(M):
                share_out[0, i, h] = st[i * ROWS : (i + 1) * ROWS]
        if b == 0:
            pl.semaphore_wait(barrier, M - 1 + G - 1 + NHEAD - 1)
        start_shares(0, b)

    row = lax.broadcasted_iota(jnp.int32, (8, W), 0)
    rate_rows = jnp.zeros((8, W), F32)
    for h in range(H):
        rate_rows = jnp.where(row == h, rates[h], rate_rows)

    def power(n):
        return jnp.exp(rate_rows * (-float(T) * n))

    for i in range(M):
        one_s[i] = power(1) * clear(g * M + i, 1)
        spread_s[0, i] = power(i) * clear(g * M, i)
        spread_s[1, i] = power(M - 1 - i) * clear(g * M + i + 1, M - 1 - i)
    for way in range(2):
        near = lax.rem(g + (G - 1 if way == 0 else 1), G)
        next_near = lax.rem(g + (G - 2 if way == 0 else 2), G)
        free = clear(near * M, M)
        coef_s[way, 0] = power(M) * free
        coef_s[way, 1] = power(2 * M) * (free * clear(next_near * M, M))

    start = jnp.full((T, W), -far, jnp.int32)
    for d in range(DOCS):
        start = jnp.where(ucol >= rel[d], rel[d], start)
    for c in range(0, T, W):
        col = lax.broadcasted_iota(jnp.int32, (T, W), 1) + c
        keep_s[:, c : c + W] = jnp.where((col >= start) & (col <= ucol), 1.0, 0.0)
    for h in range(H):
        load(2, h).wait()
        load(3, h).wait()
        g_s[h] = gain[:, h * W : (h + 1) * W] * og_s[h].astype(F32)
    lax.fori_loop(0, 3, forward, 0)
    for b in range(len(OUT_PARTS[0])):
        start_totals(0, b)
    lax.fori_loop(3, H, forward, 0)
    start_back(0)

    squares_s[...] = jnp.zeros_like(squares_s)
    dots_s[...] = jnp.zeros_like(dots_s)
    for b, (lo, hi) in enumerate(BACK_PARTS[0]):
        wait_back(0, b)
        for h in range(lo, hi):
            inc = whole(0, h)
            inc_s[h] = inc
            att = att_s[h] + wi_s[h] * dot(q_s[h], inc, NN)
            att_s[h] = att
            squares_s[...] += att * att
            dots_s[...] += g_s[h] * att

    def halves(x):
        high = x.astype(BF16)
        return [high, (x - high.astype(F32)).astype(BF16)]

    terms = jnp.concatenate(halves(squares_s[...]) + halves(dots_s[...]), axis=1)
    row = lax.broadcasted_iota(jnp.int32, (8, 4 * W), 0)
    lane = lax.broadcasted_iota(jnp.int32, (8, 4 * W), 1)
    pick = jnp.where((lane >= 2 * W) == (row == 1), 1.0, 0.0).astype(BF16)
    sums = dot(pick, terms, NT)
    sum_out[...] = sums[:2]

    def head_sum(k):
        return pltpu.make_async_remote_copy(
            src_ref=sum_out,
            dst_ref=sum_in.at[hd],
            send_sem=sum_ss.at[k - 1],
            recv_sem=sum_rs.at[k - 1],
            device_id=(s, lax.rem(hd + k, NHEAD)),
            device_id_type=MESH,
        )

    for k in range(1, NHEAD):
        head_sum(k).start()
    sum_in[hd] = sum_out[...]
    for k in range(1, NHEAD):
        head_sum(k).wait_recv()
    both = sum_in[0]
    for i in range(1, NHEAD):
        both = both + sum_in[i]
    inv = lax.rsqrt(both[0:1] / FEATURES + EPS)
    scale = inv * inv * inv * both[1:2] / FEATURES
    table = jnp.concatenate([inv, scale, jnp.zeros((6, T), F32)], axis=0).T
    inv = jnp.broadcast_to(table[:, 0:1], (T, W))
    scale = jnp.broadcast_to(table[:, 1:2], (T, W))

    for b, (lo, hi) in enumerate(OUT_PARTS[1]):
        for h in range(lo, hi):
            d_s[h] = (inv * g_s[h] - att_s[h] * scale).astype(BF16)
            gr = dot(qt_s[h], d_s[h], NN).astype(BF16)
            for i in range(M):
                share_out[1, i, h] = gr[i * ROWS : (i + 1) * ROWS]
        start_shares(1, b)

    for h in range(H):
        term = og_s[h].astype(F32) * att_s[h] * inv
        gain_mine[:, h * W : (h + 1) * W] = jnp.sum(term, axis=0, keepdims=True)

    def gain_a(o):
        return pltpu.make_async_remote_copy(
            src_ref=gain_mine,
            dst_ref=gain_in.at[m],
            send_sem=ga_ss.at[o],
            recv_sem=ga_rs.at[o],
            device_id=member(peer(o)),
            device_id_type=MESH,
        )

    def gain_b(k):
        return pltpu.make_async_remote_copy(
            src_ref=gain_tot,
            dst_ref=gain_all.at[g],
            send_sem=gb_ss.at[k - 1],
            recv_sem=gb_rs.at[k - 1],
            device_id=ally(k),
            device_id_type=MESH,
        )

    for o in range(M - 1):
        gain_a(o).start()
    gain_in[m] = gain_mine[...]

    lax.fori_loop(0, 3, backward, 0)
    for b in range(len(OUT_PARTS[1])):
        start_totals(1, b)
    for o in range(M - 1):
        gain_a(o).wait_recv()
    part = gain_in[0]
    for i in range(1, M):
        part = part + gain_in[i]
    gain_tot[...] = part
    for k in range(1, G):
        gain_b(k).start()
    gain_all[g] = part
    lax.fori_loop(3, H, backward, 0)
    start_back(1)
    for k in range(1, G):
        gain_b(k).wait_recv()
    part = gain_all[0]
    for i in range(1, G):
        part = part + gain_all[i]
    gg_ref[...] = part * (1.0 / math.sqrt(TOKENS))

    for way in range(2):
        for b in range(len(OUT_PARTS[way])):
            for o in range(M - 1):
                share(way, b, o).wait_send()
            for k in range(1, G):

                @pl.when(sends(way, k))
                def _():
                    tot(way, b, k).wait_send()

    for b in range(len(BACK_PARTS[0])):
        for o in range(M - 1):
            back(0, b, o).wait_send()
    for k in range(1, NHEAD):
        head_sum(k).wait_send()
    for o in range(M - 1):
        gain_a(o).wait_send()
    for k in range(1, G):
        gain_b(k).wait_send()

    for b, (lo, hi) in enumerate(BACK_PARTS[1]):
        wait_back(1, b)
        for h in range(lo, hi):
            out = whole(1, h)
            gk_s[:, h * W : (h + 1) * W] = (dk_s[h] + wo_s[h] * dot(v_s[h], out, NT)).astype(BF16)
            gv_s[:, h * W : (h + 1) * W] = (dv_s[h] + wo_s[h] * dot(k_s[h], out, NN)).astype(BF16)
    for b in range(len(BACK_PARTS[1])):
        for o in range(M - 1):
            back(1, b, o).wait_send()


def write(gq_s, gk_s, gv_s, gg_s, gq_hbm, gk_hbm, gv_hbm, gg_ref, sem):
    held = (gq_s, gk_s, gv_s)
    outs = (gq_hbm, gk_hbm, gv_hbm)

    def store(a, c):
        rows = slice(c * W, (c + 1) * W)
        return pltpu.make_async_copy(held[a].at[rows], outs[a].at[rows], sem.at[a, c])

    for a in range(3):
        for c in range(T // W):
            store(a, c).start()
    for h in range(H):
        gg_ref[h * W : (h + 1) * W] = gg_s[0, h * W : (h + 1) * W]
    for a in range(3):
        for c in range(T // W):
            store(a, c).wait()


def on_device(queries, keys, values, doc_lengths, decay_rates, gain, out_grad):
    hbm = pl.BlockSpec(memory_space=pltpu.HBM)
    smem = pl.BlockSpec(memory_space=pltpu.SMEM)
    vmem = pl.BlockSpec(memory_space=pltpu.VMEM)
    dma = pltpu.SemaphoreType.DMA
    wide = (H, T, W)
    shares = pltpu.VMEM((2, M, H, ROWS, W), BF16)
    block = jax.ShapeDtypeStruct((T, H * W), BF16)
    row = jax.ShapeDtypeStruct((1, H * W), F32)
    gq, gk, gv, gg = pl.pallas_call(
        kernel,
        out_shape=(
            block,
            block,
            block,
            row,
        ),
        in_specs=[hbm] * 7,
        out_specs=(vmem,) * 4,
        scratch_shapes=[
            pltpu.VMEM(wide, BF16),
            pltpu.VMEM(wide, BF16),
            pltpu.VMEM(wide, BF16),
            pltpu.VMEM(wide, BF16),
            pltpu.VMEM((H, T, T), BF16),
            pltpu.VMEM((T, T), BF16),
            pltpu.VMEM((T, T), F32),
            pltpu.VMEM(wide, F32),
            pltpu.VMEM(wide, F32),
            pltpu.VMEM(wide, F32),
            pltpu.VMEM(wide, F32),
            pltpu.VMEM(wide, F32),
            pltpu.VMEM(wide, F32),
            pltpu.VMEM(wide, BF16),
            pltpu.VMEM((H, W, T), BF16),
            pltpu.VMEM((H, W, W), BF16),
            pltpu.VMEM((T, W), F32),
            pltpu.VMEM((T, W), F32),
            pltpu.VMEM((M, 8, W), F32),
            pltpu.VMEM((2, 2, 8, W), F32),
            pltpu.VMEM((2, M, 8, W), F32),
            shares,
            shares,
            pltpu.VMEM((2, H, ROWS, W), BF16),
            pltpu.VMEM((2, G - 1, H, ROWS, W), BF16),
            pltpu.VMEM((H, ROWS, W), F32),
            pltpu.VMEM((M, H, ROWS, W), F32),
            shares,
            shares,
            pltpu.VMEM((2, T), F32),
            pltpu.VMEM((NHEAD, 2, T), F32),
            pltpu.VMEM((1, H * W), F32),
            pltpu.VMEM((M, 1, H * W), F32),
            pltpu.VMEM((1, H * W), F32),
            pltpu.VMEM((G, 1, H * W), F32),
            pltpu.SMEM((DOCS,), jnp.int32),
            pltpu.SMEM((H,), F32),
            pltpu.VMEM((1, H * W), F32),
            dma((3,)),
            dma((4, H)),
            dma((2, PARTS, M - 1)),
            dma((2, PARTS, M - 1)),
            dma((2, PARTS, G - 1)),
            dma((2, PARTS, G - 1)),
            dma((2, PARTS, M - 1)),
            dma((2, PARTS, M - 1)),
            dma((NHEAD - 1,)),
            dma((NHEAD - 1,)),
            dma((M - 1,)),
            dma((M - 1,)),
            dma((G - 1,)),
            dma((G - 1,)),
        ],
        compiler_params=pltpu.CompilerParams(
            collective_id=0, has_side_effects=True, vmem_limit_bytes=51 << 20
        ),
        cost_estimate=pl.CostEstimate(
            flops=2 * H * (6 * T * T * W + 5 * T * W * W),
            bytes_accessed=4 * T * H * W * 2,
            transcendentals=4 * H * T * W,
        ),
    )(doc_lengths, decay_rates, gain.reshape(1, H * W), queries, keys, values, out_grad)
    gq, gk, gv, gg = pl.pallas_call(
        write,
        out_shape=(block, block, block, jax.ShapeDtypeStruct((H * W,), F32)),
        in_specs=[vmem] * 4,
        out_specs=(hbm, hbm, hbm, vmem),
        scratch_shapes=[dma((3, T // W))],
        compiler_params=pltpu.CompilerParams(vmem_limit_bytes=51 << 20),
        cost_estimate=pl.CostEstimate(
            flops=0, bytes_accessed=3 * T * H * W * 2, transcendentals=0
        ),
    )(gq, gk, gv, gg)
    return gq, gk, gv, gg


def solution(mesh):
    return jax.shard_map(
        on_device,
        mesh=mesh,
        in_specs=(
            P("seq", "head"),
            P("seq", "head"),
            P("seq", "head"),
            P(),
            P("head"),
            P("head"),
            P("seq", "head"),
        ),
        out_specs=(P("seq", "head"), P("seq", "head"), P("seq", "head"), P("head")),
        check_vma=False,
    )
```

```python
import math

import jax
import jax.numpy as jnp
from jax import lax
from jax.experimental import pallas as pl
from jax.experimental.pallas import tpu as pltpu
from jax.sharding import PartitionSpec as P

EPS = 1e-06
MESH = pl.DeviceIdType.MESH
F32 = jnp.float32
BF16 = jnp.bfloat16
NT = (((1,), (1,)), ((), ()))
TN = (((0,), (0,)), ((), ()))
NN = (((1,), (0,)), ((), ()))

T = 512
HALF = T // 2
W = 128
H = 6
FEATURES = 6144
TOKENS = 16384
SEQ = 32
M = 8
G = SEQ // M
NX = 4
OFFSETS = ((1, 2), (1, 1), (1, 3), (1, 0), (0, 2), (0, 1), (0, 3))
FAR_FIRST = (2, 3, 1)
OUT_PARTS = (((0, 4), (4, 6)), ((0, 4), (4, 6)))
BACK_PARTS = (((0, 4), (4, 6)), ((0, 4), (4, 6)))
PARTS = 2
ROWS = W // M
NHEAD = 8
DOCS = 32


def dot(a, b, dims):
    return lax.dot_general(a, b, dims, preferred_element_type=F32)


def kernel(
    docs_hbm,
    rates_hbm,
    gain_hbm,
    q_hbm,
    k_hbm,
    v_hbm,
    og_hbm,
    gq_s,
    gk_s,
    gv_s,
    gg_ref,
    q_s,
    k_s,
    v_s,
    og_s,
    w_s,
    dw_s,
    keep_s,
    wi_s,
    wo_s,
    g_s,
    dk_s,
    dv_s,
    att_s,
    d_s,
    qt_s,
    inc_s,
    squares_s,
    dots_s,
    one_s,
    coef_s,
    spread_s,
    share_out,
    share_in,
    tot_out,
    tot_in,
    carry_s,
    loc_s,
    back_out,
    back_in,
    sum_out,
    sum_in,
    gain_mine,
    gain_in,
    gain_tot,
    gain_all,
    docs,
    rates,
    gain,
    small_sem,
    in_sem,
    share_ss,
    share_rs,
    tot_ss,
    tot_rs,
    back_ss,
    back_rs,
    sum_ss,
    sum_rs,
    ga_ss,
    ga_rs,
    gb_ss,
    gb_rs,
):
    s = lax.axis_index("seq")
    hd = lax.axis_index("head")
    g = s // M
    m = lax.rem(s, M)

    def member(i):
        return (g * M + i, hd)

    def peer(o):
        dz, dx = OFFSETS[o]
        return lax.rem(m // NX + dz, 2) * NX + lax.rem(lax.rem(m, NX) + dx, NX)

    def place(group, i):
        return lax.rem(i + jnp.where(group >= G // 2, NX, 0), M)

    mine = place(g, m)

    def ally(k):
        other = lax.rem(g + k, G)
        return (other * M + place(other, mine), hd)

    barrier = pltpu.get_barrier_semaphore()
    reached = [member(peer(o)) for o in range(M - 1)]
    reached = reached[:3] + [ally(k) for k in FAR_FIRST] + reached[3:]
    reached += [(s, lax.rem(hd + k, NHEAD)) for k in (4, 5, 3, 2, 6, 1, 7)]
    for device in reached:
        pl.semaphore_signal(barrier, inc=1, device_id=device, device_id_type=MESH)

    hbm = (k_hbm, v_hbm, q_hbm, og_hbm)
    vmem = (k_s, v_s, q_s, og_s)

    def load(a, h):
        return pltpu.make_async_copy(
            hbm[a].at[:, h * W : (h + 1) * W], vmem[a].at[h], in_sem.at[a, h]
        )

    small = [
        pltpu.make_async_copy(src, dst, small_sem.at[i])
        for i, (src, dst) in enumerate(((docs_hbm, docs), (rates_hbm, rates), (gain_hbm, gain)))
    ]
    for copy in small:
        copy.start()
    for h in range(H):
        load(0, h).start()
        load(1, h).start()
    for h in range(H):
        load(2, h).start()
        load(3, h).start()

    for copy in small:
        copy.wait()
    begin = s * T
    far = jnp.int32(1 << 24)
    total = jnp.int32(0)
    bits = jnp.int32(0)
    first_end = far
    last_start = -far
    rel = []
    for d in range(DOCS):
        total = total + docs[d]
        here = total - begin
        rel.append(here)
        if d < DOCS - 1:
            bits = bits | lax.shift_left(jnp.int32(1), lax.shift_right_logical(total, 9))
        first_end = jnp.where((here >= 0) & (first_end == far), here, first_end)
        last_start = jnp.where(here <= T - 1, here, last_start)

    def clear(at, count):
        if count == 0:
            return jnp.float32(1.0)
        field = lax.shift_right_logical(bits, at) & jnp.int32((1 << count) - 1)
        return jnp.where(field == 0, jnp.float32(1.0), jnp.float32(0.0))

    ucol = lax.broadcasted_iota(jnp.int32, (T, W), 0)
    ucol_f = ucol.astype(F32)
    urow_f = lax.broadcasted_iota(jnp.int32, (1, T), 1).astype(F32)

    def mask_of(r, lo, c):
        er = jnp.exp(-r * ucol_f[lo:])
        er = jnp.concatenate([er, er], axis=1)
        ek = jnp.exp(r * urow_f[:, c : c + HALF])
        return er * ek * keep_s[lo:, c : c + HALF]

    def share(way, b, o):
        to = peer(o)
        heads = slice(*OUT_PARTS[way][b])
        return pltpu.make_async_remote_copy(
            src_ref=share_out.at[way, place(g, to), heads],
            dst_ref=share_in.at[way, m, heads],
            send_sem=share_ss.at[way, b, o],
            recv_sem=share_rs.at[way, b, o],
            device_id=member(to),
            device_id_type=MESH,
        )

    def back(way, b, o):
        to = peer(o)
        heads = slice(*BACK_PARTS[way][b])
        return pltpu.make_async_remote_copy(
            src_ref=back_out.at[way, to, heads],
            dst_ref=back_in.at[way, mine, heads],
            send_sem=back_ss.at[way, b, o],
            recv_sem=back_rs.at[way, b, o],
            device_id=member(to),
            device_id_type=MESH,
        )

    def tot(way, b, k):
        heads = slice(*OUT_PARTS[way][b])
        return pltpu.make_async_remote_copy(
            src_ref=tot_out.at[way, heads],
            dst_ref=tot_in.at[way, k - 1, heads],
            send_sem=tot_ss.at[way, b, k - 1],
            recv_sem=tot_rs.at[way, b, k - 1],
            device_id=ally(k if way == 0 else G - k),
            device_id_type=MESH,
        )

    def sends(way, k):
        return g + k < G if way == 0 else g - k >= 0

    def receives(way, k):
        return g - k >= 0 if way == 0 else g + k < G

    def start_shares(way, b):
        for o in range(M - 1):
            share(way, b, o).start()
        for h in range(*OUT_PARTS[way][b]):
            share_in[way, m, h] = share_out[way, mine, h]

    def start_totals(way, b):
        for o in reversed(range(M - 1)):
            share(way, b, o).wait_recv()
        for h in range(*OUT_PARTS[way][b]):
            run = jnp.zeros((ROWS, W), F32)
            for i in range(M) if way == 0 else reversed(range(M)):
                loc_s[i, h] = run
                run = run * one_s[i, h : h + 1] + share_in[way, i, h].astype(F32)
            tot_out[way, h] = run.astype(BF16)
        for k in FAR_FIRST:

            @pl.when(sends(way, k))
            def _():
                tot(way, b, k).start()

    def gather_carry(way, b):
        for h in range(*OUT_PARTS[way][b]):
            carry_s[h] = jnp.zeros((ROWS, W), F32)
        for k in reversed(FAR_FIRST):

            @pl.when(receives(way, k))
            def _():
                tot(way, b, k).wait_recv()
                for h in range(*OUT_PARTS[way][b]):
                    term = tot_in[way, k - 1, h].astype(F32)
                    if k > 1:
                        term = term * coef_s[way, k - 2, h : h + 1]
                    carry_s[h] = carry_s[h] + term

    def start_back(way):
        ready = 0
        for b, (lo, hi) in enumerate(BACK_PARTS[way]):
            while ready < len(OUT_PARTS[way]) and OUT_PARTS[way][ready][0] < hi:
                gather_carry(way, ready)
                ready += 1
            for h in range(lo, hi):
                carry = carry_s[h]
                for i in range(M):
                    back_out[way, i, h] = (
                        loc_s[i, h] + carry * spread_s[way, i, h : h + 1]
                    ).astype(BF16)
            for o in range(M - 1):
                back(way, b, o).start()
            for h in range(lo, hi):
                back_in[way, mine, h] = back_out[way, m, h]

    def wait_back(way, b):
        for o in reversed(range(M - 1)):
            back(way, b, o).wait_recv()

    def whole(way, h):
        return back_in[way, :, h].reshape(W, W)

    def forward(h, _):
        r = rates[h]
        for c in (0, HALF):
            scores = dot(q_s[h, c:], k_s[h, c : c + HALF], NT)
            w_s[h, c:, c : c + HALF] = (scores * mask_of(r, c, c)).astype(BF16)
        att_s[h, :HALF] = dot(w_s[h, :HALF, :HALF], v_s[h, :HALF], NN)
        att_s[h, HALF:] = dot(w_s[h, HALF:], v_s[h], NN)
        w_in = jnp.where(ucol < first_end, jnp.exp(-r * (ucol_f + 1.0)), 0.0)
        wi_s[h] = w_in
        qt_s[h] = (q_s[h].astype(F32) * w_in).astype(BF16).T
        return 0

    def backward(h, _):
        r = rates[h]
        for c in (0, HALF):
            dw = dot(d_s[h, c:], v_s[h, c : c + HALF], NT)
            dw_s[c:, c : c + HALF] = (dw * mask_of(r, c, c)).astype(BF16)
        far_q = wi_s[h] * dot(d_s[h], inc_s[h], NT)
        cols = pl.ds(pl.multiple_of(h * W, W), W)
        gq_s[:HALF, cols] = (
            dot(dw_s[:HALF, :HALF], k_s[h, :HALF], NN) + far_q[:HALF]
        ).astype(BF16)
        gq_s[HALF:, cols] = (dot(dw_s[HALF:], k_s[h], NN) + far_q[HALF:]).astype(BF16)
        dk_s[h, :HALF] = dot(dw_s[:, :HALF], q_s[h], TN)
        dk_s[h, HALF:] = dot(dw_s[HALF:, HALF:], q_s[h, HALF:], TN)
        dv_s[h, :HALF] = dot(w_s[h, :, :HALF], d_s[h], TN)
        dv_s[h, HALF:] = dot(w_s[h, HALF:, HALF:], d_s[h, HALF:], TN)
        return 0

    for b, (lo, hi) in enumerate(OUT_PARTS[0]):
        for h in range(lo, hi):
            load(0, h).wait()
            load(1, h).wait()
            w_out = jnp.where(
                ucol >= last_start, jnp.exp(-rates[h] * (T - 1.0 - ucol_f)), 0.0
            )
            wo_s[h] = w_out
            ks = (k_s[h].astype(F32) * w_out).astype(BF16)
            st = dot(ks, v_s[h], TN).astype(BF16)
            for i in range(M):
                share_out[0, i, h] = st[i * ROWS : (i + 1) * ROWS]
        if b == 0:
            pl.semaphore_wait(barrier, M - 1 + G - 1 + NHEAD - 1)
        start_shares(0, b)

    row = lax.broadcasted_iota(jnp.int32, (8, W), 0)
    rate_rows = jnp.zeros((8, W), F32)
    for h in range(H):
        rate_rows = jnp.where(row == h, rates[h], rate_rows)

    def power(n):
        return jnp.exp(rate_rows * (-float(T) * n))

    for i in range(M):
        one_s[i] = power(1) * clear(g * M + i, 1)
        spread_s[0, i] = power(i) * clear(g * M, i)
        spread_s[1, i] = power(M - 1 - i) * clear(g * M + i + 1, M - 1 - i)
    for way in range(2):
        near = lax.rem(g + (G - 1 if way == 0 else 1), G)
        next_near = lax.rem(g + (G - 2 if way == 0 else 2), G)
        free = clear(near * M, M)
        coef_s[way, 0] = power(M) * free
        coef_s[way, 1] = power(2 * M) * (free * clear(next_near * M, M))

    start = jnp.full((T, W), -far, jnp.int32)
    for d in range(DOCS):
        start = jnp.where(ucol >= rel[d], rel[d], start)
    for c in range(0, T, W):
        col = lax.broadcasted_iota(jnp.int32, (T, W), 1) + c
        keep_s[:, c : c + W] = jnp.where((col >= start) & (col <= ucol), 1.0, 0.0)
    for h in range(H):
        load(2, h).wait()
        load(3, h).wait()
        g_s[h] = gain[:, h * W : (h + 1) * W] * og_s[h].astype(F32)
    lax.fori_loop(0, 3, forward, 0)
    for b in range(len(OUT_PARTS[0])):
        start_totals(0, b)
    lax.fori_loop(3, H, forward, 0)
    start_back(0)

    squares_s[...] = jnp.zeros_like(squares_s)
    dots_s[...] = jnp.zeros_like(dots_s)
    for b, (lo, hi) in enumerate(BACK_PARTS[0]):
        wait_back(0, b)
        for h in range(lo, hi):
            inc_s[h] = whole(0, h)
        for c in range(0, T, HALF):
            rows = slice(c, c + HALF)
            squares = squares_s[rows]
            dots = dots_s[rows]
            for h in range(lo, hi):
                far_att = dot(q_s[h, rows], inc_s[h], NN)
                att = att_s[h, rows] + wi_s[h, rows] * far_att
                att_s[h, rows] = att
                squares = squares + att * att
                dots = dots + g_s[h, rows] * att
            squares_s[rows] = squares
            dots_s[rows] = dots

    def halves(x):
        high = x.astype(BF16)
        return [high, (x - high.astype(F32)).astype(BF16)]

    terms = jnp.concatenate(halves(squares_s[...]) + halves(dots_s[...]), axis=1)
    row = lax.broadcasted_iota(jnp.int32, (8, 4 * W), 0)
    lane = lax.broadcasted_iota(jnp.int32, (8, 4 * W), 1)
    pick = jnp.where((lane >= 2 * W) == (row == 1), 1.0, 0.0).astype(BF16)
    sums = dot(pick, terms, NT)
    sum_out[...] = sums[:2]

    def head_sum(k):
        return pltpu.make_async_remote_copy(
            src_ref=sum_out,
            dst_ref=sum_in.at[hd],
            send_sem=sum_ss.at[k - 1],
            recv_sem=sum_rs.at[k - 1],
            device_id=(s, lax.rem(hd + k, NHEAD)),
            device_id_type=MESH,
        )

    for k in range(1, NHEAD):
        head_sum(k).start()
    sum_in[hd] = sum_out[...]
    for k in range(1, NHEAD):
        head_sum(k).wait_recv()
    both = sum_in[0]
    for i in range(1, NHEAD):
        both = both + sum_in[i]
    inv = lax.rsqrt(both[0:1] / FEATURES + EPS)
    scale = inv * inv * inv * both[1:2] / FEATURES
    table = jnp.concatenate([inv, scale, jnp.zeros((6, T), F32)], axis=0).T
    inv = jnp.broadcast_to(table[:, 0:1], (T, W))
    scale = jnp.broadcast_to(table[:, 1:2], (T, W))

    for b, (lo, hi) in enumerate(OUT_PARTS[1]):
        for h in range(lo, hi):
            d_s[h] = (inv * g_s[h] - att_s[h] * scale).astype(BF16)
            gr = dot(qt_s[h], d_s[h], NN).astype(BF16)
            for i in range(M):
                share_out[1, i, h] = gr[i * ROWS : (i + 1) * ROWS]
        start_shares(1, b)

    for h in range(H):
        term = og_s[h].astype(F32) * att_s[h] * inv
        gain_mine[:, h * W : (h + 1) * W] = jnp.sum(term, axis=0, keepdims=True)

    def gain_a(o):
        return pltpu.make_async_remote_copy(
            src_ref=gain_mine,
            dst_ref=gain_in.at[m],
            send_sem=ga_ss.at[o],
            recv_sem=ga_rs.at[o],
            device_id=member(peer(o)),
            device_id_type=MESH,
        )

    def gain_b(k):
        return pltpu.make_async_remote_copy(
            src_ref=gain_tot,
            dst_ref=gain_all.at[g],
            send_sem=gb_ss.at[k - 1],
            recv_sem=gb_rs.at[k - 1],
            device_id=ally(k),
            device_id_type=MESH,
        )

    for o in range(M - 1):
        gain_a(o).start()
    gain_in[m] = gain_mine[...]

    lax.fori_loop(0, 3, backward, 0)
    for b in range(len(OUT_PARTS[1])):
        start_totals(1, b)
    for o in range(M - 1):
        gain_a(o).wait_recv()
    part = gain_in[0]
    for i in range(1, M):
        part = part + gain_in[i]
    gain_tot[...] = part
    for k in range(1, G):
        gain_b(k).start()
    gain_all[g] = part
    lax.fori_loop(3, H, backward, 0)
    start_back(1)
    for k in range(1, G):
        gain_b(k).wait_recv()
    part = gain_all[0]
    for i in range(1, G):
        part = part + gain_all[i]
    gg_ref[...] = part * (1.0 / math.sqrt(TOKENS))

    for way in range(2):
        for b in range(len(OUT_PARTS[way])):
            for o in range(M - 1):
                share(way, b, o).wait_send()
            for k in range(1, G):

                @pl.when(sends(way, k))
                def _():
                    tot(way, b, k).wait_send()

    for b in range(len(BACK_PARTS[0])):
        for o in range(M - 1):
            back(0, b, o).wait_send()
    for k in range(1, NHEAD):
        head_sum(k).wait_send()
    for o in range(M - 1):
        gain_a(o).wait_send()
    for k in range(1, G):
        gain_b(k).wait_send()

    for b, (lo, hi) in enumerate(BACK_PARTS[1]):
        wait_back(1, b)
        for h in range(lo, hi):
            out = whole(1, h)
            gk_s[:, h * W : (h + 1) * W] = (dk_s[h] + wo_s[h] * dot(v_s[h], out, NT)).astype(BF16)
            gv_s[:, h * W : (h + 1) * W] = (dv_s[h] + wo_s[h] * dot(k_s[h], out, NN)).astype(BF16)
    for b in range(len(BACK_PARTS[1])):
        for o in range(M - 1):
            back(1, b, o).wait_send()


def write(gq_s, gk_s, gv_s, gg_s, gq_hbm, gk_hbm, gv_hbm, gg_ref, sem):
    held = (gq_s, gk_s, gv_s)
    outs = (gq_hbm, gk_hbm, gv_hbm)
    copies = [pltpu.make_async_copy(held[a], outs[a], sem.at[a]) for a in range(3)]
    for copy in copies:
        copy.start()
    for h in range(H):
        gg_ref[h * W : (h + 1) * W] = gg_s[0, h * W : (h + 1) * W]
    for copy in copies:
        copy.wait()


def on_device(queries, keys, values, doc_lengths, decay_rates, gain, out_grad):
    hbm = pl.BlockSpec(memory_space=pltpu.HBM)
    smem = pl.BlockSpec(memory_space=pltpu.SMEM)
    vmem = pl.BlockSpec(memory_space=pltpu.VMEM)
    dma = pltpu.SemaphoreType.DMA
    wide = (H, T, W)
    shares = pltpu.VMEM((2, M, H, ROWS, W), BF16)
    block = jax.ShapeDtypeStruct((T, H * W), BF16)
    row = jax.ShapeDtypeStruct((1, H * W), F32)
    gq, gk, gv, gg = pl.pallas_call(
        kernel,
        out_shape=(
            block,
            block,
            block,
            row,
        ),
        in_specs=[hbm] * 7,
        out_specs=(vmem,) * 4,
        scratch_shapes=[
            pltpu.VMEM(wide, BF16),
            pltpu.VMEM(wide, BF16),
            pltpu.VMEM(wide, BF16),
            pltpu.VMEM(wide, BF16),
            pltpu.VMEM((H, T, T), BF16),
            pltpu.VMEM((T, T), BF16),
            pltpu.VMEM((T, T), F32),
            pltpu.VMEM(wide, F32),
            pltpu.VMEM(wide, F32),
            pltpu.VMEM(wide, F32),
            pltpu.VMEM(wide, F32),
            pltpu.VMEM(wide, F32),
            pltpu.VMEM(wide, F32),
            pltpu.VMEM(wide, BF16),
            pltpu.VMEM((H, W, T), BF16),
            pltpu.VMEM((H, W, W), BF16),
            pltpu.VMEM((T, W), F32),
            pltpu.VMEM((T, W), F32),
            pltpu.VMEM((M, 8, W), F32),
            pltpu.VMEM((2, 2, 8, W), F32),
            pltpu.VMEM((2, M, 8, W), F32),
            shares,
            shares,
            pltpu.VMEM((2, H, ROWS, W), BF16),
            pltpu.VMEM((2, G - 1, H, ROWS, W), BF16),
            pltpu.VMEM((H, ROWS, W), F32),
            pltpu.VMEM((M, H, ROWS, W), F32),
            shares,
            shares,
            pltpu.VMEM((2, T), F32),
            pltpu.VMEM((NHEAD, 2, T), F32),
            pltpu.VMEM((1, H * W), F32),
            pltpu.VMEM((M, 1, H * W), F32),
            pltpu.VMEM((1, H * W), F32),
            pltpu.VMEM((G, 1, H * W), F32),
            pltpu.SMEM((DOCS,), jnp.int32),
            pltpu.SMEM((H,), F32),
            pltpu.VMEM((1, H * W), F32),
            dma((3,)),
            dma((4, H)),
            dma((2, PARTS, M - 1)),
            dma((2, PARTS, M - 1)),
            dma((2, PARTS, G - 1)),
            dma((2, PARTS, G - 1)),
            dma((2, PARTS, M - 1)),
            dma((2, PARTS, M - 1)),
            dma((NHEAD - 1,)),
            dma((NHEAD - 1,)),
            dma((M - 1,)),
            dma((M - 1,)),
            dma((G - 1,)),
            dma((G - 1,)),
        ],
        compiler_params=pltpu.CompilerParams(
            collective_id=0, has_side_effects=True, vmem_limit_bytes=51 << 20
        ),
        cost_estimate=pl.CostEstimate(
            flops=2 * H * (6 * T * T * W + 5 * T * W * W),
            bytes_accessed=4 * T * H * W * 2,
            transcendentals=4 * H * T * W,
        ),
    )(doc_lengths, decay_rates, gain.reshape(1, H * W), queries, keys, values, out_grad)
    gq, gk, gv, gg = pl.pallas_call(
        write,
        out_shape=(block, block, block, jax.ShapeDtypeStruct((H * W,), F32)),
        in_specs=[vmem] * 4,
        out_specs=(hbm, hbm, hbm, vmem),
        scratch_shapes=[dma((3,))],
        compiler_params=pltpu.CompilerParams(vmem_limit_bytes=51 << 20),
        cost_estimate=pl.CostEstimate(
            flops=0, bytes_accessed=3 * T * H * W * 2, transcendentals=0
        ),
    )(gq, gk, gv, gg)
    return gq, gk, gv, gg


def solution(mesh):
    return jax.shard_map(
        on_device,
        mesh=mesh,
        in_specs=(
            P("seq", "head"),
            P("seq", "head"),
            P("seq", "head"),
            P(),
            P("head"),
            P("head"),
            P("seq", "head"),
        ),
        out_specs=(P("seq", "head"), P("seq", "head"), P("seq", "head"), P("head")),
        check_vma=False,
    )
```
